128 devices in a mesh: gx: 8 (over x_hi, y), gy: 16 (over z, x_lo, core).
Axes of the slice: x: 4 (x_hi: 2, x_lo: 2; x = x_hi * 2 + x_lo), y: 4, z: 4, core: 2. Of those that a mesh axis runs over, the one named last changes fastest.
Arguments:
- terminal_value: float32 [32768, 2048], P('gx', 'gy'), may hold values from -0.5 to 0.9
- running_cost: float32 [32768, 2048], P('gx', 'gy'), may hold values from 0.1 to 1
- density: float32 [4, 32768, 2048], P(None, 'gx', 'gy'), may hold values from 0.5 to 5
- first_taps: float32 [33], replicated, may hold values from 0.005 to 0.05
- second_taps: float32 [33], replicated, may hold values from 0.005 to 0.05
Outputs:
- value_field: float32 [32768, 2048], P('gx', 'gy')
The draws below stay inside these ranges and needn't reach their ends.
All inputs are finite; a program needn't handle non-finite values.
Results may differ from the reference program's by a relative error of at most 0.00002.
Values sent between devices are 32-bit elements; how exact they have to be, the bound alone decides.
A program may use at most 128 MiB of HBM per device.

```python
import math
import jax
import jax.numpy as jnp
from jax import lax

STEPS = 4
KR = 16
KW = 33
NX = 32768
NY = 2048


def draw_terminal_value(key, part):
    key = jax.random.fold_in(key, 11)
    return jax.random.uniform(key, (NX, NY), jnp.float32, -0.5, 0.5)


def block_scale(own_key, shape, shards, smallest, largest):
    loudness = 1.0
    for dim, parts in shards:
        heights = jax.random.uniform(jax.random.fold_in(jax.random.fold_in(own_key, 6), dim), (parts,), jnp.float32, smallest / len(shards), largest / len(shards))
        loudness = loudness * jnp.repeat(jnp.exp(heights), shape[dim] // parts).reshape((-1,) + (1,) * (len(shape) - 1 - dim))
    return loudness


def setup_inputs(seed: int = 0) -> dict:
    key_list = jax.random.split(jax.random.key(seed), 6)
    return {
        "terminal_value": draw_terminal_value(jax.random.fold_in(key_list[5], 71), 0),
        "running_cost": jnp.clip(jnp.exp(math.log(1.0) - 2.3025851 * jax.random.uniform(key_list[1], (NX, NY), jnp.float32) ** block_scale(key_list[1], (NX, NY), ((0, 8), (1, 16)), -0.2, 0.2)), 0.1, 1.0),
        "density": jnp.clip(jnp.exp(math.log(5.0) - 2.3025851 * jax.random.uniform(key_list[2], (STEPS, NX, NY), jnp.float32) ** block_scale(key_list[2], (STEPS, NX, NY), ((1, 8), (2, 16)), -0.2, 0.2)), 0.5, 5.0),
        "first_taps": jnp.clip(jnp.exp(jax.random.uniform(key_list[3], (KW,), jnp.float32, math.log(0.005), math.log(0.05))), 0.005, 0.05),
        "second_taps": jnp.clip(jnp.exp(jax.random.uniform(key_list[4], (KW,), jnp.float32, math.log(0.005), math.log(0.05))), 0.005, 0.05),
    }


time_step = 0.1
viscosity = 2.0


def tap_sum(extended, kernel, along_dim, length):
    accumulated = kernel[0] * lax.slice_in_dim(extended, 0, length, axis=along_dim)
    for offset in range(1, kernel.shape[0]):
        accumulated = accumulated + kernel[offset] * lax.slice_in_dim(extended, offset, offset + length, axis=along_dim)
    return accumulated


def hjb_update(center, upper_cells, lower_cells, left_cells, right_cells, step_cost):
    back_rows = center - upper_cells
    fore_rows = lower_cells - center
    back_cols = center - left_cells
    fore_cols = right_cells - center
    rise_rows = jnp.maximum(back_rows, 0.0)
    fall_rows = jnp.minimum(fore_rows, 0.0)
    rise_cols = jnp.maximum(back_cols, 0.0)
    fall_cols = jnp.minimum(fore_cols, 0.0)
    hamiltonian = 0.5 * (rise_rows * rise_rows + fall_rows * fall_rows + rise_cols * rise_cols + fall_cols * fall_cols)
    laplacian = (fore_rows - back_rows) + (fore_cols - back_cols)
    return center + time_step * (viscosity * laplacian - hamiltonian + step_cost)


def reference(terminal_value, running_cost, density, first_taps, second_taps):
    def congestion_of(field):
        padded = jnp.pad(field, ((KR, KR), (0, 0)), mode="wrap")
        blurred = tap_sum(padded, first_taps, 0, NX)
        padded = jnp.pad(blurred, ((0, 0), (KR, KR)), mode="wrap")
        return tap_sum(padded, second_taps, 1, NY)

    def advance(current, field):
        step_cost = running_cost + congestion_of(field)
        updated = hjb_update(current, jnp.roll(current, 1, 0), jnp.roll(current, -1, 0),
                             jnp.roll(current, 1, 1), jnp.roll(current, -1, 1), step_cost)
        return updated, None

    value_field, unused = lax.scan(advance, terminal_value, density, reverse=True)
    return value_field
```

```python
import functools

import jax
import jax.numpy as jnp
from jax import lax
from jax.experimental import pallas as pl
from jax.experimental.pallas import tpu as pltpu
from jax.sharding import PartitionSpec as P

MESH = pl.DeviceIdType.MESH
F32 = jnp.float32
BF16 = jnp.bfloat16
STEPS = 4
ROWS = 4096
UNIT = 1024
UNITS = ROWS // UNIT
HALF = 512
TAPS = 33
REACH = 16
LAG = 2
SLOTS = STEPS * UNITS
PIECES = ((0, 1008), (1008, 1088), (2096, 1024), (3120, 976))


def split(x):
    hi = x.astype(BF16)
    lo = (x - hi.astype(F32)).astype(BF16)
    return hi, lo


def toeplitz(index, taps_ref, first, last, scale):
    def add(t, acc):
        return jnp.where(index == t, taps_ref[t] * scale, acc)

    return lax.fori_loop(first, last, add, jnp.zeros(index.shape, F32))


def build_rows(taps_ref, lhs):
    pos = lax.broadcasted_iota(jnp.int32, (64, 128), 0)
    col = lax.broadcasted_iota(jnp.int32, (64, 128), 1)
    row = (pos % 8) * 8 + pos // 8
    hi, lo = split(toeplitz(col - row, taps_ref, 0, TAPS, 1.0))
    lhs[0:64, 0:128] = hi
    lhs[0:64, 128:256] = hi
    lhs[64:128, 0:128] = lo
    lhs[64:128, 128:256] = jnp.zeros((64, 128), BF16)


def build_cols(taps_ref, own):
    src = lax.broadcasted_iota(jnp.int32, (128, 128), 0)
    dst = lax.broadcasted_iota(jnp.int32, (128, 128), 1)
    hi, lo = split(toeplitz(src - dst + REACH, taps_ref, 0, TAPS, 0.005))
    own[0:128, 0:128] = hi
    own[0:128, 128:256] = lo
    own[128:256, 0:128] = hi
    own[128:256, 128:256] = jnp.zeros((128, 128), BF16)


def build_halo(taps_ref, halo_hi, halo_lo):
    lam = lax.broadcasted_iota(jnp.int32, (128, 256), 0)
    nu = lax.broadcasted_iota(jnp.int32, (128, 256), 1)
    out_part = nu // 128
    place = (nu % 128 + 16) % 128
    out_q, out_e = place // 32, place % 32
    upper = lam % 32 >= 16
    shifted = (lam + 16) % 128
    q = jnp.where(upper, shifted // 32, lam // 32)
    m = jnp.where(upper, shifted % 32, lam % 32)
    part = jnp.where(upper, 0, 1)
    fits = (part == out_part) & (q == out_q) & (out_e >= 16)
    index = jnp.where(fits, m - (out_e - 16), -1)
    hi, lo = split(toeplitz(index, taps_ref, 0, 16, 0.005))
    halo_hi[0:128, :] = hi
    halo_lo[0:128, :] = lo
    m = jnp.where(upper, lam % 32 - 16, lam % 32)
    part = jnp.where(upper, 1, 0)
    fits = (part == out_part) & (lam // 32 == out_q) & (out_e < 16)
    index = jnp.where(fits, 32 + m - out_e, -1)
    hi, lo = split(toeplitz(index, taps_ref, 17, TAPS, 0.005))
    halo_hi[128:256, :] = hi
    halo_lo[128:256, :] = lo


def pack_edges(u, lane):
    a = jnp.where((lane[:32] == 127) | (lane[:32] < 1), u[:32], pltpu.roll(u[32:], 2, 1))
    b = jnp.where((lane[:16] == 127) | (lane[:16] < 3), a[:16], pltpu.roll(a[16:], 4, 1))
    return jnp.where((lane[:8] == 127) | (lane[:8] < 7), b[:8], pltpu.roll(b[8:], 8, 1))


def unpack_edges(mixed, window):
    parts = []
    for k in range(8):
        shift = 16 * window + 2 * (k // 4) + 4 * (k // 2 % 2) + 8 * (k % 2)
        parts.append(pltpu.roll(mixed, (128 - shift) % 128, 1) if shift else mixed)
    return jnp.concatenate(parts, axis=0)


def place_edges(packed, window, acc, lane):
    if window == 0:
        return packed
    low = 16 * window - 1
    here = (lane[:8] >= low) & (lane[:8] < low + 16)
    return jnp.where(here, pltpu.roll(packed, 16 * window, 1), acc)


def kernel(
    gx, gy, t1, t2, term, cost, dens, out,
    x, rc, tv, u, c, hs, hr, es, er, pe, yb, lhs, own, halo_hi, halo_lo,
    x_load, c_load, t_load, x_send, x_recv, h_send, h_recv, e_send, e_recv, r_send, r_recv,
):
    ix, iy = lax.axis_index("gx"), lax.axis_index("gy")
    up, down = lax.rem(ix + gx - 1, gx), lax.rem(ix + 1, gx)
    left, right = lax.rem(iy + gy - 1, gy), lax.rem(iy + 1, gy)
    ids = ({"gx": up}, {"gx": down}, {"gy": left}, {"gy": right})
    barrier = pltpu.get_barrier_semaphore()
    for place in ids:
        pl.semaphore_signal(barrier, inc=1, device_id=place, device_id_type=MESH)

    def load(f, unit):
        start, size = PIECES[unit]
        return pltpu.make_async_copy(
            dens.at[f, pl.ds(start, size)], x.at[f, pl.ds(start + REACH, size)], x_load.at[f, unit]
        )

    def load_cost(unit):
        rows = pl.ds(unit * UNIT, UNIT)
        return pltpu.make_async_copy(cost.at[rows], rc.at[rows], c_load.at[unit])

    def load_term(unit):
        rows = pl.ds(unit * UNIT, UNIT)
        return pltpu.make_async_copy(term.at[rows], tv.at[rows], t_load.at[unit])

    def remote(src, dst, send, recv, place):
        return pltpu.make_async_remote_copy(
            src_ref=src, dst_ref=dst, send_sem=send, recv_sem=recv, device_id=place, device_id_type=MESH
        )

    def rows_up(f):
        return remote(
            dens.at[f, pl.ds(0, REACH)], x.at[f, pl.ds(REACH + ROWS, REACH)],
            x_send.at[f, 0], x_recv.at[f, 0], {"gx": up},
        )

    def rows_down(f):
        return remote(
            dens.at[f, pl.ds(ROWS - REACH, REACH)], x.at[f, pl.ds(0, REACH)],
            x_send.at[f, 1], x_recv.at[f, 1], {"gx": down},
        )

    def halo(f, chunk, side):
        return remote(
            hs.at[f, chunk, side], hr.at[f, chunk, side],
            h_send.at[f, chunk, side], h_recv.at[f, chunk, side], {"gy": (right, left)[side]},
        )

    def edge(n, unit, side):
        return remote(
            es.at[n, unit, side], er.at[n, unit, side],
            e_send.at[n, unit, side], e_recv.at[n, unit, side], {"gy": (right, left)[side]},
        )

    def value_up(n):
        return remote(
            u.at[n, pl.ds(8, 8)], u.at[n, pl.ds(8 + ROWS, 8)], r_send.at[n, 0], r_recv.at[n, 0], {"gx": up}
        )

    def value_down(n):
        return remote(
            u.at[n, pl.ds(ROWS, 8)], u.at[n, pl.ds(0, 8)], r_send.at[n, 1], r_recv.at[n, 1], {"gx": down}
        )

    def fetch(slot):
        f = STEPS - 1 - slot // UNITS
        for unit in range(UNITS):
            @pl.when((slot + 1) % UNITS == unit)
            def _():
                load(f, unit).start()

                @pl.when(slot < UNITS)
                def _():
                    load_cost(unit).start()
                    load_term(slot).start()

    for slot in range(2):
        load(STEPS - 1, slot + 1).start()
        load_cost(slot + 1).start()
        load_term(slot).start()
    for f in range(STEPS):
        x[f, ROWS + 2 * REACH:, :] = jnp.zeros((32, 128), F32)
    build_rows(t1, lhs)
    build_cols(t2, own)
    build_halo(t2, halo_hi, halo_lo)
    pl.semaphore_wait(barrier, 4)
    for f in range(STEPS - 1, -1, -1):
        rows_up(f).start()
        rows_down(f).start()

    lane = lax.broadcasted_iota(jnp.int32, (64, 128), 1)
    sub = lax.broadcasted_iota(jnp.int32, (8, 128), 0)
    odd = lane[:8] % 2 == 1

    def blur(f, chunk):
        base = pl.multiple_of(chunk * HALF, HALF)
        a = b = None
        for group in range(2):
            hi, lo = split(x[f, pl.ds(base + group * 256, 320), :])
            for pair in range(2):
                at = pair * 128
                rhs = jnp.concatenate(
                    [
                        jnp.concatenate([hi[at:at + 128], lo[at:at + 128]], axis=0),
                        jnp.concatenate([hi[at + 64:at + 192], lo[at + 64:at + 192]], axis=0),
                    ],
                    axis=1,
                )
                both = jnp.dot(lhs[...], rhs, preferred_element_type=F32)
                both = both[:64] + both[64:]
                p = 2 * group + pair
                y0, y1 = both[:, :128], both[:, 128:]
                for i, y in enumerate((y0, y1)):
                    hi_y, lo_y = split(y)
                    yb[p * 128 + i * 64:p * 128 + i * 64 + 64, 0:128] = hi_y
                    yb[p * 128 + i * 64:p * 128 + i * 64 + 64, 128:256] = lo_y
                if p == 0:
                    a, b = y0, y1
                else:
                    here = (lane >= 32 * p - 16) & (lane < 32 * p + 16)
                    a = jnp.where(here, pltpu.roll(y0, 32 * p, 1), a)
                    b = jnp.where(here, pltpu.roll(y1, 32 * p, 1), b)
        b = pltpu.roll(b, 16, 1)
        high = lane % 32 >= 16
        hs[f, chunk, 0] = jnp.where(high, a, b)
        hs[f, chunk, 1] = jnp.where(high, b, a)
        halo(f, chunk, 0).start()
        halo(f, chunk, 1).start()
        for part in range(4):
            o = jnp.dot(yb[part * 128:part * 128 + 128, :], own[...], preferred_element_type=F32)
            o = o[:, :128] + o[:, 128:]
            for k in range(16):
                at = base + part * 128 + k // 8 * 64
                r = rc[pl.ds(at + k % 8, 8, stride=8), :]
                c[f, pl.ds(base + part * 128 + k * 8, 8), :] = o[k * 8:k * 8 + 8] + 0.005 * r

    def send_values(n, unit):
        p0, p1 = pe[0], pltpu.roll(pe[1], 1, 1)
        es[n, unit, 0] = jnp.where(odd, p0, p1)
        es[n, unit, 1] = jnp.where(odd, p1, p0)
        edge(n, unit, 0).start()
        edge(n, unit, 1).start()

        @pl.when(unit == 0)
        def _():
            value_up(n).start()

        @pl.when(unit == UNITS - 1)
        def _():
            value_down(n).start()

    def start_values(unit):
        for h in range(2):
            acc = None
            for w in range(8):
                at = unit * UNIT + h * HALF + w * 64
                v = jnp.concatenate([tv[pl.ds(at + k, 8, stride=8), :] for k in range(8)], axis=0) * 0.05
                u[0, pl.ds(pl.multiple_of(8 + at, 8), 64), :] = v
                acc = place_edges(pack_edges(v, lane), w, acc, lane)
            pe[h] = acc
        send_values(0, unit)

    def step_half(f, n, unit, h):
        chunk = unit * 2 + h
        halo(f, chunk, 0).wait_recv()
        halo(f, chunk, 1).wait_recv()
        hi, lo = split(jnp.concatenate([hr[f, chunk, 0], hr[f, chunk, 1]], axis=1))
        o = jnp.dot(jnp.concatenate([hi, lo], axis=0), halo_hi[...], preferred_element_type=F32)
        o = o[:64] + o[64:] + jnp.dot(hi, halo_lo[...], preferred_element_type=F32)
        from_left, from_right = er[n, unit, 0], er[n, unit, 1]
        if h == 0:
            mixed = jnp.where(odd, pltpu.roll(from_right, 127, 1), pltpu.roll(from_left, 1, 1))
        else:
            mixed = jnp.where(odd, pltpu.roll(from_right, 126, 1), from_left)
        ends = (lane < 16) | (lane >= 112)
        acc = None
        for w in range(8):
            at = pl.multiple_of(chunk * HALF + w * 64, 64)
            p = w // 2
            share = o[:, w % 2 * 128:w % 2 * 128 + 128]
            if p:
                share = pltpu.roll(share, 128 - 32 * p, 1)
            v = u[n, pl.ds(8 + at, 64), :]
            before = u[n, pl.ds(at, 8), :]
            after = u[n, pl.ds(72 + at, 8), :]
            first = jnp.where(sub == 0, pltpu.roll(before, 1, 0), pltpu.roll(v[56:], 1, 0))
            last = jnp.where(sub == 7, pltpu.roll(after, 7, 0), pltpu.roll(v[:8], 7, 0))
            sides = unpack_edges(mixed, w)
            new = v + c[f, pl.ds(at, 64), :] + jnp.where(ends, share, 0.0)
            back = v - jnp.concatenate([first, v[:56]], axis=0)
            new = new - back * jnp.maximum(back + 0.2, 0.2)
            fore = jnp.concatenate([v[8:], last], axis=0) - v
            new = new + fore * jnp.maximum(0.2 - fore, 0.2)
            back = v - jnp.where(lane == 0, sides, pltpu.roll(v, 1, 1))
            new = new - back * jnp.maximum(back + 0.2, 0.2)
            fore = jnp.where(lane == 127, sides, pltpu.roll(v, 127, 1)) - v
            new = new + fore * jnp.maximum(0.2 - fore, 0.2)
            u[n + 1, pl.ds(8 + at, 64), :] = new
            acc = place_edges(pack_edges(new, lane), w, acc, lane)
        pe[h] = acc

    def step(f, n, unit):
        edge(n, unit, 0).wait_recv()
        edge(n, unit, 1).wait_recv()

        @pl.when(unit == 0)
        def _():
            value_down(n).wait_recv()

        @pl.when(unit == UNITS - 1)
        def _():
            value_up(n).wait_recv()

        step_half(f, n, unit, 0)
        step_half(f, n, unit, 1)

        @pl.when(f > 0)
        def _():
            send_values(n + 1, unit)

        @pl.when(f == 0)
        def _():
            def finish(w, carry):
                at = unit * UNIT + w * 64
                v = u[STEPS, pl.ds(pl.multiple_of(8 + at, 8), 64), :] * 20.0
                for k in range(8):
                    out[pl.ds(at + k, 8, stride=8), :] = v[k * 8:k * 8 + 8]
                return carry

            lax.fori_loop(0, UNIT // 64, finish, 0)

    def slot_body(slot, carry):
        @pl.when(slot < SLOTS)
        def _():
            f = STEPS - 1 - slot // UNITS
            unit = (slot + 1) % UNITS

            @pl.when(slot + 2 < SLOTS)
            def _():
                fetch(slot + 2)

            for k in range(UNITS):
                @pl.when(unit == k)
                def _():
                    load(f, k).wait()

            @pl.when(slot < UNITS)
            def _():
                load_cost(unit).wait()
                load_term(slot).wait()

            @pl.when(unit == UNITS - 1)
            def _():
                rows_up(f).wait_recv()

            @pl.when(unit == 0)
            def _():
                rows_down(f).wait_recv()

            def half(h, carry):
                blur(f, unit * 2 + h)
                return carry

            lax.fori_loop(0, 2, half, 0)

            @pl.when(slot < UNITS)
            def _():
                start_values(slot)

        @pl.when(slot >= LAG)
        def _():
            late = slot - LAG
            n = late // UNITS
            step(STEPS - 1 - n, n, (late + 1) % UNITS)

        return carry

    lax.fori_loop(0, SLOTS + LAG, slot_body, 0)

    for f in range(STEPS):
        rows_up(f).wait_send()
        rows_down(f).wait_send()
        value_up(f).wait_send()
        value_down(f).wait_send()

    def drain(i, carry):
        f, chunk = i // 8, i % 8
        halo(f, chunk, 0).wait_send()
        halo(f, chunk, 1).wait_send()
        return carry

    lax.fori_loop(0, STEPS * 8, drain, 0)

    def drain_edges(i, carry):
        edge(i // UNITS, i % UNITS, 0).wait_send()
        edge(i // UNITS, i % UNITS, 1).wait_send()
        return carry

    lax.fori_loop(0, STEPS * UNITS, drain_edges, 0)


def solution(mesh):
    gx, gy = mesh.shape["gx"], mesh.shape["gy"]

    def shards(terminal_value, running_cost, density, first_taps, second_taps):
        dma = pltpu.SemaphoreType.DMA
        smem = pl.BlockSpec(memory_space=pltpu.SMEM)
        hbm = pl.BlockSpec(memory_space=pl.ANY)
        return pl.pallas_call(
            functools.partial(kernel, gx, gy),
            name="sweep",
            out_shape=jax.ShapeDtypeStruct((ROWS, 128), F32),
            in_specs=[smem, smem, hbm, hbm, hbm],
            out_specs=pl.BlockSpec(memory_space=pltpu.VMEM),
            scratch_shapes=[
                pltpu.VMEM((STEPS, ROWS + 64, 128), F32),
                pltpu.VMEM((ROWS, 128), F32),
                pltpu.VMEM((ROWS, 128), F32),
                pltpu.VMEM((STEPS + 1, ROWS + 16, 128), F32),
                pltpu.VMEM((STEPS, ROWS, 128), F32),
                pltpu.VMEM((STEPS, 8, 2, 64, 128), F32),
                pltpu.VMEM((STEPS, 8, 2, 64, 128), F32),
                pltpu.VMEM((STEPS, UNITS, 2, 8, 128), F32),
                pltpu.VMEM((STEPS, UNITS, 2, 8, 128), F32),
                pltpu.VMEM((2, 8, 128), F32),
                pltpu.VMEM((HALF, 256), BF16),
                pltpu.VMEM((128, 256), BF16),
                pltpu.VMEM((256, 256), BF16),
                pltpu.VMEM((256, 256), BF16),
                pltpu.VMEM((256, 256), BF16),
                dma((STEPS, UNITS)), dma((UNITS,)), dma((UNITS,)),
                dma((STEPS, 2)), dma((STEPS, 2)),
                dma((STEPS, 8, 2)), dma((STEPS, 8, 2)),
                dma((STEPS, UNITS, 2)), dma((STEPS, UNITS, 2)),
                dma((STEPS, 2)), dma((STEPS, 2)),
            ],
            compiler_params=pltpu.CompilerParams(
                collective_id=0, has_side_effects=True, vmem_limit_bytes=56 * 1024 * 1024
            ),
        )(first_taps, second_taps, terminal_value, running_cost, density)

    placed = (P("gx", "gy"), P("gx", "gy"), P(None, "gx", "gy"), P(), P())
    return jax.shard_map(shards, mesh=mesh, in_specs=placed, out_specs=P("gx", "gy"), check_vma=False)
```

```python
import functools

import jax
import jax.numpy as jnp
from jax import lax
from jax.experimental import pallas as pl
from jax.experimental.pallas import tpu as pltpu
from jax.sharding import PartitionSpec as P

MESH = pl.DeviceIdType.MESH
F32 = jnp.float32
BF16 = jnp.bfloat16
STEPS = 4
ROWS = 4096
UNIT = 1024
UNITS = ROWS // UNIT
HALF = 512
TAPS = 33
REACH = 16
LAG = 4
SLOTS = STEPS * UNITS
PIECES = ((0, 1008), (1008, 1088), (2096, 1024), (3120, 976))


def split(x):
    hi = x.astype(BF16)
    lo = (x - hi.astype(F32)).astype(BF16)
    return hi, lo


def toeplitz(index, taps_ref, first, last, scale):
    def add(t, acc):
        return jnp.where(index == t, taps_ref[t] * scale, acc)

    return lax.fori_loop(first, last, add, jnp.zeros(index.shape, F32))


def build_rows(taps_ref, lhs):
    pos = lax.broadcasted_iota(jnp.int32, (64, 128), 0)
    col = lax.broadcasted_iota(jnp.int32, (64, 128), 1)
    row = (pos % 8) * 8 + pos // 8
    hi, lo = split(toeplitz(col - row, taps_ref, 0, TAPS, 1.0))
    lhs[0:64, 0:128] = hi
    lhs[0:64, 128:256] = hi
    lhs[64:128, 0:128] = lo
    lhs[64:128, 128:256] = jnp.zeros((64, 128), BF16)


def build_cols(taps_ref, own):
    src = lax.broadcasted_iota(jnp.int32, (128, 128), 0)
    dst = lax.broadcasted_iota(jnp.int32, (128, 128), 1)
    hi, lo = split(toeplitz(src - dst + REACH, taps_ref, 0, TAPS, 0.005))
    own[0:128, 0:128] = hi
    own[0:128, 128:256] = lo
    own[128:256, 0:128] = hi
    own[128:256, 128:256] = jnp.zeros((128, 128), BF16)


def build_halo(taps_ref, halo_hi, halo_lo):
    lam = lax.broadcasted_iota(jnp.int32, (128, 256), 0)
    nu = lax.broadcasted_iota(jnp.int32, (128, 256), 1)
    out_part = nu // 128
    place = (nu % 128 + 16) % 128
    out_q, out_e = place // 32, place % 32
    upper = lam % 32 >= 16
    shifted = (lam + 16) % 128
    q = jnp.where(upper, shifted // 32, lam // 32)
    m = jnp.where(upper, shifted % 32, lam % 32)
    part = jnp.where(upper, 0, 1)
    fits = (part == out_part) & (q == out_q) & (out_e >= 16)
    index = jnp.where(fits, m - (out_e - 16), -1)
    hi, lo = split(toeplitz(index, taps_ref, 0, 16, 0.005))
    halo_hi[0:128, :] = hi
    halo_lo[0:128, :] = lo
    m = jnp.where(upper, lam % 32 - 16, lam % 32)
    part = jnp.where(upper, 1, 0)
    fits = (part == out_part) & (lam // 32 == out_q) & (out_e < 16)
    index = jnp.where(fits, 32 + m - out_e, -1)
    hi, lo = split(toeplitz(index, taps_ref, 17, TAPS, 0.005))
    halo_hi[128:256, :] = hi
    halo_lo[128:256, :] = lo


def kernel(
    gx, gy, t1, t2, term, cost, dens, out,
    x, rc, tv, u, c, hs, hr, es, er, yb, lhs, own, halo_hi, halo_lo,
    x_load, c_load, t_load, x_send, x_recv, h_send, h_recv, e_send, e_recv, r_send, r_recv, o_store,
):
    ix, iy = lax.axis_index("gx"), lax.axis_index("gy")
    up, down = lax.rem(ix + gx - 1, gx), lax.rem(ix + 1, gx)
    left, right = lax.rem(iy + gy - 1, gy), lax.rem(iy + 1, gy)
    ids = ({"gx": up}, {"gx": down}, {"gy": left}, {"gy": right})
    barrier = pltpu.get_barrier_semaphore()
    for place in ids:
        pl.semaphore_signal(barrier, inc=1, device_id=place, device_id_type=MESH)

    def load(f, unit):
        start, size = PIECES[unit]
        return pltpu.make_async_copy(
            dens.at[f, pl.ds(start, size)], x.at[f, pl.ds(start + REACH, size)], x_load.at[f, unit]
        )

    def load_cost(unit):
        rows = pl.ds(unit * UNIT, UNIT)
        return pltpu.make_async_copy(cost.at[rows], rc.at[rows], c_load.at[unit])

    def load_term(unit):
        rows = pl.ds(unit * UNIT, UNIT)
        return pltpu.make_async_copy(term.at[rows], tv.at[rows], t_load.at[unit])

    def store(unit):
        rows = pl.ds(pl.multiple_of(unit * UNIT, UNIT), UNIT)
        return pltpu.make_async_copy(tv.at[rows], out.at[rows], o_store.at[unit])

    def remote(src, dst, send, recv, place):
        return pltpu.make_async_remote_copy(
            src_ref=src, dst_ref=dst, send_sem=send, recv_sem=recv, device_id=place, device_id_type=MESH
        )

    def rows_up(f):
        return remote(
            dens.at[f, pl.ds(0, REACH)], x.at[f, pl.ds(REACH + ROWS, REACH)],
            x_send, x_recv.at[f, 0], {"gx": up},
        )

    def rows_down(f):
        return remote(
            dens.at[f, pl.ds(ROWS - REACH, REACH)], x.at[f, pl.ds(0, REACH)],
            x_send, x_recv.at[f, 1], {"gx": down},
        )

    def halo(f, unit, side):
        return remote(
            hs.at[f, unit, side], hr.at[f, unit, side],
            h_send, h_recv.at[f, unit, side], {"gy": (right, left)[side]},
        )

    def edge(n, unit, side):
        return remote(
            es.at[n, unit, side], er.at[n, unit, side],
            e_send, e_recv.at[n, unit, side], {"gy": (right, left)[side]},
        )

    def value_up(n):
        return remote(
            u.at[n, pl.ds(8, 8)], u.at[n, pl.ds(8 + ROWS, 8)], r_send, r_recv.at[n, 0], {"gx": up}
        )

    def value_down(n):
        return remote(
            u.at[n, pl.ds(ROWS, 8)], u.at[n, pl.ds(0, 8)], r_send, r_recv.at[n, 1], {"gx": down}
        )

    def fetch(slot):
        f = STEPS - 1 - slot // UNITS
        for unit in range(UNITS):
            @pl.when((slot + 1) % UNITS == unit)
            def _():
                load(f, unit).start()

                @pl.when(slot < UNITS)
                def _():
                    load_cost(unit).start()
                    load_term(slot).start()

    for slot in range(2):
        load(STEPS - 1, slot + 1).start()
        load_cost(slot + 1).start()
        load_term(slot).start()
    for f in range(STEPS):
        x[f, ROWS + 2 * REACH:, :] = jnp.zeros((32, 128), F32)
    build_rows(t1, lhs)
    build_cols(t2, own)
    build_halo(t2, halo_hi, halo_lo)
    pl.semaphore_wait(barrier, 4)
    for f in range(STEPS - 1, -1, -1):
        rows_up(f).start()
        rows_down(f).start()

    lane = lax.broadcasted_iota(jnp.int32, (64, 128), 1)
    sub = lax.broadcasted_iota(jnp.int32, (8, 128), 0)

    def blur(f, unit, h):
        base = pl.multiple_of(unit * UNIT + h * HALF, HALF)
        a = b = None
        for group in range(2):
            hi, lo = split(x[f, pl.ds(base + group * 256, 320), :])
            for pair in range(2):
                at = pair * 128
                rhs = jnp.concatenate(
                    [
                        jnp.concatenate([hi[at:at + 128], lo[at:at + 128]], axis=0),
                        jnp.concatenate([hi[at + 64:at + 192], lo[at + 64:at + 192]], axis=0),
                    ],
                    axis=1,
                )
                both = jnp.dot(lhs[...], rhs, preferred_element_type=F32)
                both = both[:64] + both[64:]
                p = 2 * group + pair
                y0, y1 = both[:, :128], both[:, 128:]
                for i, y in enumerate((y0, y1)):
                    hi_y, lo_y = split(y)
                    yb[p * 128 + i * 64:p * 128 + i * 64 + 64, 0:128] = hi_y
                    yb[p * 128 + i * 64:p * 128 + i * 64 + 64, 128:256] = lo_y
                if p == 0:
                    a, b = y0, y1
                else:
                    here = (lane >= 32 * p - 16) & (lane < 32 * p + 16)
                    a = jnp.where(here, pltpu.roll(y0, 32 * p, 1), a)
                    b = jnp.where(here, pltpu.roll(y1, 32 * p, 1), b)
        b = pltpu.roll(b, 16, 1)
        high = lane % 32 >= 16
        at = pl.ds(pl.multiple_of(h * 64, 64), 64)
        hs[f, unit, 0, at, :] = jnp.where(high, a, b)
        hs[f, unit, 1, at, :] = jnp.where(high, b, a)
        for part in range(4):
            o = jnp.dot(yb[part * 128:part * 128 + 128, :], own[...], preferred_element_type=F32)
            o = o[:, :128] + o[:, 128:]
            for k in range(16):
                at = base + part * 128 + k // 8 * 64
                r = rc[pl.ds(at + k % 8, 8, stride=8), :]
                c[f, pl.ds(base + part * 128 + k * 8, 8), :] = o[k * 8:k * 8 + 8] + 0.005 * r

    def send_values(n, unit):
        for b in range(8):
            at = pl.multiple_of(8 + unit * UNIT + b * 128, 8)
            turned = u[n, pl.ds(at, 128), :].T
            es[n, unit, 0, b:b + 1, :] = turned[127:]
            es[n, unit, 1, b:b + 1, :] = turned[:1]
        edge(n, unit, 0).start()
        edge(n, unit, 1).start()

        @pl.when(unit == 0)
        def _():
            value_up(n).start()

        @pl.when(unit == UNITS - 1)
        def _():
            value_down(n).start()

    def start_values(unit):
        for w in range(UNIT // 64):
            at = unit * UNIT + w * 64
            v = jnp.concatenate([tv[pl.ds(at + k, 8, stride=8), :] for k in range(8)], axis=0) * 0.05
            u[0, pl.ds(pl.multiple_of(8 + at, 8), 64), :] = v
        send_values(0, unit)

    def step_half(f, n, unit, h):
        at = pl.ds(pl.multiple_of(h * 64, 64), 64)
        hi, lo = split(jnp.concatenate([hr[f, unit, 0, at, :], hr[f, unit, 1, at, :]], axis=1))
        o = jnp.dot(jnp.concatenate([hi, lo], axis=0), halo_hi[...], preferred_element_type=F32)
        o = o[:64] + o[64:] + jnp.dot(hi, halo_lo[...], preferred_element_type=F32)
        ends = (lane < 16) | (lane >= 112)
        for w in range(8):
            at = pl.multiple_of(unit * UNIT + h * HALF + w * 64, 64)
            p = w // 2
            if w % 2 == 0:
                block = h * 4 + p
                turned = jnp.concatenate(
                    [
                        jnp.broadcast_to(er[n, unit, side, pl.ds(block, 1), :], (64, 128))
                        for side in range(2)
                    ],
                    axis=0,
                ).T
            share = o[:, w % 2 * 128:w % 2 * 128 + 128]
            if p:
                share = pltpu.roll(share, 128 - 32 * p, 1)
            v = u[n, pl.ds(8 + at, 64), :]
            before = u[n, pl.ds(at, 8), :]
            after = u[n, pl.ds(72 + at, 8), :]
            first = jnp.where(sub == 0, pltpu.roll(before, 1, 0), pltpu.roll(v[56:], 1, 0))
            last = jnp.where(sub == 7, pltpu.roll(after, 7, 0), pltpu.roll(v[:8], 7, 0))
            sides = turned[w % 2 * 64:w % 2 * 64 + 64]
            new = v + c[f, pl.ds(at, 64), :] + jnp.where(ends, share, 0.0)
            back = v - jnp.concatenate([first, v[:56]], axis=0)
            new = new - back * jnp.maximum(back + 0.2, 0.2)
            fore = jnp.concatenate([v[8:], last], axis=0) - v
            new = new + fore * jnp.maximum(0.2 - fore, 0.2)
            back = v - jnp.where(lane == 0, sides, pltpu.roll(v, 1, 1))
            new = new - back * jnp.maximum(back + 0.2, 0.2)
            fore = jnp.where(lane == 127, sides, pltpu.roll(v, 127, 1)) - v
            new = new + fore * jnp.maximum(0.2 - fore, 0.2)
            u[n + 1, pl.ds(8 + at, 64), :] = new

    def step(f, n, unit):
        for side in range(2):
            edge(n, unit, side).wait_recv()
            halo(f, unit, side).wait_recv()

        @pl.when(unit == 0)
        def _():
            value_down(n).wait_recv()

        @pl.when(unit == UNITS - 1)
        def _():
            value_up(n).wait_recv()

        step_half(f, n, unit, 0)
        step_half(f, n, unit, 1)

        @pl.when(f > 0)
        def _():
            send_values(n + 1, unit)

        @pl.when(f == 0)
        def _():
            for w in range(UNIT // 64):
                at = unit * UNIT + w * 64
                v = u[STEPS, pl.ds(pl.multiple_of(8 + at, 8), 64), :] * 20.0
                for k in range(8):
                    tv[pl.ds(at + k, 8, stride=8), :] = v[k * 8:k * 8 + 8]
            store(unit).start()

    def slot_body(slot, carry):
        @pl.when(slot < SLOTS)
        def _():
            f = STEPS - 1 - slot // UNITS
            unit = (slot + 1) % UNITS

            @pl.when(slot + 2 < SLOTS)
            def _():
                fetch(slot + 2)

            for k in range(UNITS):
                @pl.when(unit == k)
                def _():
                    load(f, k).wait()

            @pl.when(slot < UNITS)
            def _():
                load_cost(unit).wait()
                load_term(slot).wait()

            @pl.when(unit == UNITS - 1)
            def _():
                rows_up(f).wait_recv()

            @pl.when(unit == 0)
            def _():
                rows_down(f).wait_recv()

            def half(h, carry):
                blur(f, unit, h)
                return carry

            lax.fori_loop(0, 2, half, 0)
            halo(f, unit, 0).start()
            halo(f, unit, 1).start()

            @pl.when(slot < UNITS)
            def _():
                start_values(slot)

        @pl.when(slot >= LAG)
        def _():
            late = slot - LAG
            n = late // UNITS
            step(STEPS - 1 - n, n, (late + 1) % UNITS)

        return carry

    lax.fori_loop(0, SLOTS + LAG, slot_body, 0)

    remote(x.at[0, pl.ds(0, 128)], x.at[0, pl.ds(0, 128)], x_send, x_recv.at[0, 0], ids[0]).wait_send()
    remote(x.at[0, pl.ds(0, 64)], x.at[0, pl.ds(0, 64)], r_send, r_recv.at[0, 0], ids[0]).wait_send()
    remote(hs, hr, h_send, h_recv.at[0, 0, 0], ids[2]).wait_send()
    remote(es, er, e_send, e_recv.at[0, 0, 0], ids[2]).wait_send()
    for unit in range(UNITS):
        store(unit).wait()


def solution(mesh):
    gx, gy = mesh.shape["gx"], mesh.shape["gy"]

    def shards(terminal_value, running_cost, density, first_taps, second_taps):
        dma = pltpu.SemaphoreType.DMA
        smem = pl.BlockSpec(memory_space=pltpu.SMEM)
        hbm = pl.BlockSpec(memory_space=pl.ANY)
        return pl.pallas_call(
            functools.partial(kernel, gx, gy),
            name="sweep",
            out_shape=jax.ShapeDtypeStruct((ROWS, 128), F32),
            in_specs=[smem, smem, hbm, hbm, hbm],
            out_specs=hbm,
            scratch_shapes=[
                pltpu.VMEM((STEPS, ROWS + 64, 128), F32),
                pltpu.VMEM((ROWS, 128), F32),
                pltpu.VMEM((ROWS, 128), F32),
                pltpu.VMEM((STEPS + 1, ROWS + 16, 128), F32),
                pltpu.VMEM((STEPS, ROWS, 128), F32),
                pltpu.VMEM((STEPS, UNITS, 2, 128, 128), F32),
                pltpu.VMEM((STEPS, UNITS, 2, 128, 128), F32),
                pltpu.VMEM((STEPS, UNITS, 2, 8, 128), F32),
                pltpu.VMEM((STEPS, UNITS, 2, 8, 128), F32),
                pltpu.VMEM((HALF, 256), BF16),
                pltpu.VMEM((128, 256), BF16),
                pltpu.VMEM((256, 256), BF16),
                pltpu.VMEM((256, 256), BF16),
                pltpu.VMEM((256, 256), BF16),
                dma((STEPS, UNITS)), dma((UNITS,)), dma((UNITS,)),
                dma, dma((STEPS, 2)),
                dma, dma((STEPS, UNITS, 2)),
                dma, dma((STEPS, UNITS, 2)),
                dma, dma((STEPS, 2)),
                dma((UNITS,)),
            ],
            compiler_params=pltpu.CompilerParams(
                collective_id=0, has_side_effects=True, vmem_limit_bytes=56 * 1024 * 1024
            ),
        )(first_taps, second_taps, terminal_value, running_cost, density)

    placed = (P("gx", "gy"), P("gx", "gy"), P(None, "gx", "gy"), P(), P())
    return jax.shard_map(shards, mesh=mesh, in_specs=placed, out_specs=P("gx", "gy"), check_vma=False)
```

```python
import functools

import jax
import jax.numpy as jnp
from jax import lax
from jax.experimental import pallas as pl
from jax.experimental.pallas import tpu as pltpu
from jax.sharding import PartitionSpec as P

MESH = pl.DeviceIdType.MESH
F32 = jnp.float32
BF16 = jnp.bfloat16
STEPS = 4
ROWS = 4096
UNIT = 1024
UNITS = ROWS // UNIT
HALF = 512
TAPS = 33
REACH = 16
LAG = 4
COPIES = 8
SLOTS = STEPS * UNITS
PIECES = ((0, 1008), (1008, 1088), (2096, 1024), (3120, 976))


def split(x):
    hi = x.astype(BF16)
    lo = (x - hi.astype(F32)).astype(BF16)
    return hi, lo


def toeplitz(index, taps_ref, first, last, scale):
    def add(t, acc):
        return jnp.where(index == t, taps_ref[t] * scale, acc)

    return lax.fori_loop(first, last, add, jnp.zeros(index.shape, F32))


def build_rows(taps_ref, lhs):
    pos = lax.broadcasted_iota(jnp.int32, (64, 128), 0)
    col = lax.broadcasted_iota(jnp.int32, (64, 128), 1)
    row = (pos % 8) * 8 + pos // 8
    hi, lo = split(toeplitz(col - row, taps_ref, 0, TAPS, 1.0))
    lhs[0:64, 0:128] = hi
    lhs[0:64, 128:256] = hi
    lhs[64:128, 0:128] = lo
    lhs[64:128, 128:256] = jnp.zeros((64, 128), BF16)


def build_cols(taps_ref, own):
    src = lax.broadcasted_iota(jnp.int32, (128, 128), 0)
    dst = lax.broadcasted_iota(jnp.int32, (128, 128), 1)
    hi, lo = split(toeplitz(src - dst + REACH, taps_ref, 0, TAPS, 0.005))
    own[0:128, 0:128] = hi
    own[0:128, 128:256] = lo
    own[128:256, 0:128] = hi
    own[128:256, 128:256] = jnp.zeros((128, 128), BF16)


def build_halo(taps_ref, halo_hi, halo_lo):
    lam = lax.broadcasted_iota(jnp.int32, (128, 256), 0)
    nu = lax.broadcasted_iota(jnp.int32, (128, 256), 1)
    out_part = nu // 128
    place = (nu % 128 + 16) % 128
    out_q, out_e = place // 32, place % 32
    upper = lam % 32 >= 16
    shifted = (lam + 16) % 128
    q = jnp.where(upper, shifted // 32, lam // 32)
    m = jnp.where(upper, shifted % 32, lam % 32)
    part = jnp.where(upper, 0, 1)
    fits = (part == out_part) & (q == out_q) & (out_e >= 16)
    index = jnp.where(fits, m - (out_e - 16), -1)
    hi, lo = split(toeplitz(index, taps_ref, 0, 16, 0.005))
    halo_hi[0:128, :] = hi
    halo_lo[0:128, :] = lo
    m = jnp.where(upper, lam % 32 - 16, lam % 32)
    part = jnp.where(upper, 1, 0)
    fits = (part == out_part) & (lam // 32 == out_q) & (out_e < 16)
    index = jnp.where(fits, 32 + m - out_e, -1)
    hi, lo = split(toeplitz(index, taps_ref, 17, TAPS, 0.005))
    halo_hi[128:256, :] = hi
    halo_lo[128:256, :] = lo


def kernel(
    gx, gy, t1, t2, term, cost, dens, out,
    x, rc, tv, u, c, hs, hr, es, er, yb, lhs, own, halo_hi, halo_lo,
    x_load, c_load, t_load, x_send, x_recv, h_send, h_recv, e_send, e_recv, r_send, r_recv, o_store,
):
    ix, iy = lax.axis_index("gx"), lax.axis_index("gy")
    up, down = lax.rem(ix + gx - 1, gx), lax.rem(ix + 1, gx)
    left, right = lax.rem(iy + gy - 1, gy), lax.rem(iy + 1, gy)
    ids = ({"gx": up}, {"gx": down}, {"gy": left}, {"gy": right})
    barrier = pltpu.get_barrier_semaphore()
    for place in ids:
        pl.semaphore_signal(barrier, inc=1, device_id=place, device_id_type=MESH)

    def load(f, unit):
        start, size = PIECES[unit]
        return pltpu.make_async_copy(
            dens.at[f, pl.ds(start, size)], x.at[f, pl.ds(start + REACH, size)], x_load.at[f, unit]
        )

    def load_cost(unit):
        rows = pl.ds(unit * UNIT, UNIT)
        return pltpu.make_async_copy(cost.at[rows], rc.at[rows], c_load.at[unit])

    def load_term(unit):
        rows = pl.ds(unit * UNIT, UNIT)
        return pltpu.make_async_copy(term.at[rows], tv.at[rows], t_load.at[unit])

    def store(unit):
        rows = pl.ds(pl.multiple_of(unit * UNIT, UNIT), UNIT)
        return pltpu.make_async_copy(tv.at[rows], out.at[rows], o_store.at[unit])

    def remote(src, dst, send, recv, place):
        return pltpu.make_async_remote_copy(
            src_ref=src, dst_ref=dst, send_sem=send, recv_sem=recv, device_id=place, device_id_type=MESH
        )

    def rows_up(f):
        return remote(
            dens.at[f, pl.ds(0, REACH)], x.at[f, pl.ds(REACH + ROWS, REACH)],
            x_send, x_recv.at[f, 0], {"gx": up},
        )

    def rows_down(f):
        return remote(
            dens.at[f, pl.ds(ROWS - REACH, REACH)], x.at[f, pl.ds(0, REACH)],
            x_send, x_recv.at[f, 1], {"gx": down},
        )

    def halo(f, unit, side):
        return remote(
            hs.at[f, unit, side], hr.at[f, unit, side],
            h_send, h_recv.at[f, unit, side], {"gy": (right, left)[side]},
        )

    def edge(n, unit, side):
        return remote(
            es.at[n, unit, side], er.at[n, unit, side],
            e_send, e_recv.at[n, unit, side], {"gy": (right, left)[side]},
        )

    def value_up(n):
        return remote(
            u.at[n, pl.ds(8, 8)], u.at[n, pl.ds(8 + ROWS, 8)], r_send, r_recv.at[n, 0], {"gx": up}
        )

    def value_down(n):
        return remote(
            u.at[n, pl.ds(ROWS, 8)], u.at[n, pl.ds(0, 8)], r_send, r_recv.at[n, 1], {"gx": down}
        )

    def fetch(slot):
        f = STEPS - 1 - slot // UNITS
        for unit in range(UNITS):
            @pl.when((slot + 1) % UNITS == unit)
            def _():
                load(f, unit).start()

                @pl.when(slot < UNITS)
                def _():
                    load_cost(unit).start()
                    load_term(slot).start()

    for slot in range(2):
        load(STEPS - 1, slot + 1).start()
        load_cost(slot + 1).start()
        load_term(slot).start()
    for f in range(STEPS):
        x[f, ROWS + 2 * REACH:, :] = jnp.zeros((32, 128), F32)
    build_rows(t1, lhs)
    build_cols(t2, own)
    pl.semaphore_wait(barrier, 4)
    for f in range(STEPS - 1, -1, -1):
        rows_up(f).start()
        rows_down(f).start()

    lane = lax.broadcasted_iota(jnp.int32, (64, 128), 1)
    sub = lax.broadcasted_iota(jnp.int32, (8, 128), 0)

    def blur(f, unit, h):
        base = pl.multiple_of(unit * UNIT + h * HALF, HALF)
        a = b = None
        for group in range(2):
            hi, lo = split(x[f, pl.ds(base + group * 256, 320), :])
            for pair in range(2):
                at = pair * 128
                rhs = jnp.concatenate(
                    [
                        jnp.concatenate([hi[at:at + 128], lo[at:at + 128]], axis=0),
                        jnp.concatenate([hi[at + 64:at + 192], lo[at + 64:at + 192]], axis=0),
                    ],
                    axis=1,
                )
                both = jnp.dot(lhs[...], rhs, preferred_element_type=F32)
                both = both[:64] + both[64:]
                p = 2 * group + pair
                y0, y1 = both[:, :128], both[:, 128:]
                for i, y in enumerate((y0, y1)):
                    hi_y, lo_y = split(y)
                    yb[p * 128 + i * 64:p * 128 + i * 64 + 64, 0:128] = hi_y
                    yb[p * 128 + i * 64:p * 128 + i * 64 + 64, 128:256] = lo_y
                if p == 0:
                    a, b = y0, y1
                else:
                    here = (lane >= 32 * p - 16) & (lane < 32 * p + 16)
                    a = jnp.where(here, pltpu.roll(y0, 32 * p, 1), a)
                    b = jnp.where(here, pltpu.roll(y1, 32 * p, 1), b)
        b = pltpu.roll(b, 16, 1)
        high = lane % 32 >= 16
        at = pl.ds(pl.multiple_of(h * 64, 64), 64)
        hs[f, unit, 0, at, :] = jnp.where(high, a, b)
        hs[f, unit, 1, at, :] = jnp.where(high, b, a)
        for part in range(4):
            o = jnp.dot(yb[part * 128:part * 128 + 128, :], own[...], preferred_element_type=F32)
            o = o[:, :128] + o[:, 128:]
            for k in range(16):
                at = base + part * 128 + k // 8 * 64
                r = rc[pl.ds(at + k % 8, 8, stride=8), :]
                c[f, pl.ds(base + part * 128 + k * 8, 8), :] = o[k * 8:k * 8 + 8] + 0.005 * r

    def send_values(n, unit):
        for b in range(8):
            at = pl.multiple_of(8 + unit * UNIT + b * 128, 8)
            turned = u[n, pl.ds(at, 128), :].T
            es[n, unit, 0, b:b + 1, :] = turned[127:]
            es[n, unit, 1, b:b + 1, :] = turned[:1]
        edge(n, unit, 0).start()
        edge(n, unit, 1).start()

        @pl.when(unit == 0)
        def _():
            value_up(n).start()

        @pl.when(unit == UNITS - 1)
        def _():
            value_down(n).start()

    def start_values(unit):
        for w in range(UNIT // 64):
            at = unit * UNIT + w * 64
            v = jnp.concatenate([tv[pl.ds(at + k, 8, stride=8), :] for k in range(8)], axis=0) * 0.05
            u[0, pl.ds(pl.multiple_of(8 + at, 8), 64), :] = v
        send_values(0, unit)

    def step_half(f, n, unit, h):
        at = pl.ds(pl.multiple_of(h * 64, 64), 64)
        hi, lo = split(jnp.concatenate([hr[f, unit, 0, at, :], hr[f, unit, 1, at, :]], axis=1))
        o = jnp.dot(jnp.concatenate([hi, lo], axis=0), halo_hi[...], preferred_element_type=F32)
        o = o[:64] + o[64:] + jnp.dot(hi, halo_lo[...], preferred_element_type=F32)
        ends = (lane < 16) | (lane >= 112)
        for w in range(8):
            at = pl.multiple_of(unit * UNIT + h * HALF + w * 64, 64)
            p = w // 2
            if w % 2 == 0:
                block = h * 4 + p
                turned = jnp.concatenate(
                    [
                        jnp.broadcast_to(er[n, unit, side, pl.ds(block, 1), :], (64, 128))
                        for side in range(2)
                    ],
                    axis=0,
                ).T
            share = o[:, w % 2 * 128:w % 2 * 128 + 128]
            if p:
                share = pltpu.roll(share, 128 - 32 * p, 1)
            v = u[n, pl.ds(8 + at, 64), :]
            before = u[n, pl.ds(at, 8), :]
            after = u[n, pl.ds(72 + at, 8), :]
            first = jnp.where(sub == 0, pltpu.roll(before, 1, 0), pltpu.roll(v[56:], 1, 0))
            last = jnp.where(sub == 7, pltpu.roll(after, 7, 0), pltpu.roll(v[:8], 7, 0))
            sides = turned[w % 2 * 64:w % 2 * 64 + 64]
            new = v + c[f, pl.ds(at, 64), :] + jnp.where(ends, share, 0.0)
            back = v - jnp.concatenate([first, v[:56]], axis=0)
            new = new - back * jnp.maximum(back + 0.2, 0.2)
            fore = jnp.concatenate([v[8:], last], axis=0) - v
            new = new + fore * jnp.maximum(0.2 - fore, 0.2)
            back = v - jnp.where(lane == 0, sides, pltpu.roll(v, 1, 1))
            new = new - back * jnp.maximum(back + 0.2, 0.2)
            fore = jnp.where(lane == 127, sides, pltpu.roll(v, 127, 1)) - v
            new = new + fore * jnp.maximum(0.2 - fore, 0.2)
            u[n + 1, pl.ds(8 + at, 64), :] = new

    def step(f, n, unit):
        for side in range(2):
            edge(n, unit, side).wait_recv()
            halo(f, unit, side).wait_recv()

        @pl.when(unit == 0)
        def _():
            value_down(n).wait_recv()

        @pl.when(unit == UNITS - 1)
        def _():
            value_up(n).wait_recv()

        step_half(f, n, unit, 0)
        step_half(f, n, unit, 1)

        @pl.when(f > 0)
        def _():
            send_values(n + 1, unit)

        @pl.when(f == 0)
        def _():
            for w in range(UNIT // 64):
                at = unit * UNIT + w * 64
                v = u[STEPS, pl.ds(pl.multiple_of(8 + at, 8), 64), :] * 20.0
                for k in range(8):
                    out[pl.ds(at + k, 8, stride=8), :] = v[k * 8:k * 8 + 8]

    def slot_body(slot, carry):
        @pl.when(slot < SLOTS)
        def _():
            f = STEPS - 1 - slot // UNITS
            unit = (slot + 1) % UNITS

            @pl.when(slot + 2 < SLOTS)
            def _():
                fetch(slot + 2)

            for k in range(UNITS):
                @pl.when(unit == k)
                def _():
                    load(f, k).wait()

            @pl.when(slot < UNITS)
            def _():
                load_cost(unit).wait()
                load_term(slot).wait()

            @pl.when(unit == UNITS - 1)
            def _():
                rows_up(f).wait_recv()

            @pl.when(unit == 0)
            def _():
                rows_down(f).wait_recv()

            def half(h, carry):
                blur(f, unit, h)
                return carry

            half(0, 0)
            half(1, 0)
            halo(f, unit, 0).start()
            halo(f, unit, 1).start()

            @pl.when(slot == 0)
            def _():
                build_halo(t2, halo_hi, halo_lo)

            @pl.when(slot < UNITS)
            def _():
                start_values(slot)

        @pl.when(slot >= LAG)
        def _():
            late = slot - LAG
            n = late // UNITS
            step(STEPS - 1 - n, n, (late + 1) % UNITS)

        return carry

    lax.fori_loop(0, SLOTS + LAG, slot_body, 0)

    remote(x.at[0, pl.ds(0, 128)], x.at[0, pl.ds(0, 128)], x_send, x_recv.at[0, 0], ids[0]).wait_send()
    remote(x.at[0, pl.ds(0, 64)], x.at[0, pl.ds(0, 64)], r_send, r_recv.at[0, 0], ids[0]).wait_send()
    remote(hs, hr, h_send, h_recv.at[0, 0, 0], ids[2]).wait_send()
    remote(es, er, e_send, e_recv.at[0, 0, 0], ids[2]).wait_send()


def hand_over(src, dst, sems):
    parts = []
    for i in range(COPIES):
        rows = pl.ds(i * (ROWS // COPIES), ROWS // COPIES)
        parts.append(pltpu.make_async_copy(src.at[rows], dst.at[rows], sems.at[i]))
        parts[-1].start()
    for part in parts:
        part.wait()


def solution(mesh):
    gx, gy = mesh.shape["gx"], mesh.shape["gy"]

    def shards(terminal_value, running_cost, density, first_taps, second_taps):
        dma = pltpu.SemaphoreType.DMA
        smem = pl.BlockSpec(memory_space=pltpu.SMEM)
        hbm = pl.BlockSpec(memory_space=pl.ANY)
        swept = pl.pallas_call(
            functools.partial(kernel, gx, gy),
            name="sweep",
            out_shape=pltpu.VMEM((ROWS, 128), F32),
            in_specs=[smem, smem, hbm, hbm, hbm],
            out_specs=pl.BlockSpec(memory_space=pltpu.VMEM),
            scratch_shapes=[
                pltpu.VMEM((STEPS, ROWS + 64, 128), F32),
                pltpu.VMEM((ROWS, 128), F32),
                pltpu.VMEM((ROWS, 128), F32),
                pltpu.VMEM((STEPS + 1, ROWS + 16, 128), F32),
                pltpu.VMEM((STEPS, ROWS, 128), F32),
                pltpu.VMEM((STEPS, UNITS, 2, 128, 128), F32),
                pltpu.VMEM((STEPS, UNITS, 2, 128, 128), F32),
                pltpu.VMEM((STEPS, UNITS, 2, 8, 128), F32),
                pltpu.VMEM((STEPS, UNITS, 2, 8, 128), F32),
                pltpu.VMEM((HALF, 256), BF16),
                pltpu.VMEM((128, 256), BF16),
                pltpu.VMEM((256, 256), BF16),
                pltpu.VMEM((256, 256), BF16),
                pltpu.VMEM((256, 256), BF16),
                dma((STEPS, UNITS)), dma((UNITS,)), dma((UNITS,)),
                dma, dma((STEPS, 2)),
                dma, dma((STEPS, UNITS, 2)),
                dma, dma((STEPS, UNITS, 2)),
                dma, dma((STEPS, 2)),
                dma((UNITS,)),
            ],
            compiler_params=pltpu.CompilerParams(
                collective_id=0, has_side_effects=True, vmem_limit_bytes=60 * 1024 * 1024
            ),
        )(first_taps, second_taps, terminal_value, running_cost, density)
        return pl.pallas_call(
            hand_over,
            name="hand_over",
            out_shape=jax.ShapeDtypeStruct((ROWS, 128), F32),
            in_specs=[pl.BlockSpec(memory_space=pltpu.VMEM)],
            out_specs=hbm,
            scratch_shapes=[dma((COPIES,))],
            compiler_params=pltpu.CompilerParams(vmem_limit_bytes=4 << 20),
        )(swept)

    placed = (P("gx", "gy"), P("gx", "gy"), P(None, "gx", "gy"), P(), P())
    return jax.shard_map(shards, mesh=mesh, in_specs=placed, out_specs=P("gx", "gy"), check_vma=False)
```

```python
import functools

import jax
import jax.numpy as jnp
from jax import lax
from jax.experimental import pallas as pl
from jax.experimental.pallas import tpu as pltpu
from jax.sharding import PartitionSpec as P

MESH = pl.DeviceIdType.MESH
F32 = jnp.float32
BF16 = jnp.bfloat16
STEPS = 4
ROWS = 4096
UNIT = 1024
UNITS = ROWS // UNIT
HALF = 512
TAPS = 33
REACH = 16
LAG = 4
SLOTS = STEPS * UNITS
PIECES = ((0, 1008), (1008, 1088), (2096, 1024), (3120, 976))


def split(x):
    hi = x.astype(BF16)
    lo = (x - hi.astype(F32)).astype(BF16)
    return hi, lo


def toeplitz(index, taps_ref, first, last, scale):
    def add(t, acc):
        return jnp.where(index == t, taps_ref[t] * scale, acc)

    return lax.fori_loop(first, last, add, jnp.zeros(index.shape, F32))


def build_rows(taps_ref, lhs):
    pos = lax.broadcasted_iota(jnp.int32, (64, 128), 0)
    col = lax.broadcasted_iota(jnp.int32, (64, 128), 1)
    row = (pos % 8) * 8 + pos // 8
    hi, lo = split(toeplitz(col - row, taps_ref, 0, TAPS, 1.0))
    lhs[0:64, 0:128] = hi
    lhs[0:64, 128:256] = hi
    lhs[64:128, 0:128] = lo
    lhs[64:128, 128:256] = jnp.zeros((64, 128), BF16)


def build_cols(taps_ref, own):
    src = lax.broadcasted_iota(jnp.int32, (128, 128), 0)
    dst = lax.broadcasted_iota(jnp.int32, (128, 128), 1)
    hi, lo = split(toeplitz(src - dst + REACH, taps_ref, 0, TAPS, 0.005))
    own[0:128, 0:128] = hi
    own[0:128, 128:256] = lo
    own[128:256, 0:128] = hi
    own[128:256, 128:256] = jnp.zeros((128, 128), BF16)


def build_halo(taps_ref, halo_hi, halo_lo):
    lam = lax.broadcasted_iota(jnp.int32, (128, 256), 0)
    nu = lax.broadcasted_iota(jnp.int32, (128, 256), 1)
    out_part = nu // 128
    place = (nu % 128 + 16) % 128
    out_q, out_e = place // 32, place % 32
    upper = lam % 32 >= 16
    shifted = (lam + 16) % 128
    q = jnp.where(upper, shifted // 32, lam // 32)
    m = jnp.where(upper, shifted % 32, lam % 32)
    part = jnp.where(upper, 0, 1)
    fits = (part == out_part) & (q == out_q) & (out_e >= 16)
    index = jnp.where(fits, m - (out_e - 16), -1)
    hi, lo = split(toeplitz(index, taps_ref, 0, 16, 0.005))
    halo_hi[0:128, :] = hi
    halo_lo[0:128, :] = lo
    m = jnp.where(upper, lam % 32 - 16, lam % 32)
    part = jnp.where(upper, 1, 0)
    fits = (part == out_part) & (lam // 32 == out_q) & (out_e < 16)
    index = jnp.where(fits, 32 + m - out_e, -1)
    hi, lo = split(toeplitz(index, taps_ref, 17, TAPS, 0.005))
    halo_hi[128:256, :] = hi
    halo_lo[128:256, :] = lo


def kernel(
    gx, gy, taps1, taps2, term, cost, dens, out, t1, t2, t_sem,
    x, rc, tv, u, c, hs, hr, es, er, yb, lhs, own, halo_hi, halo_lo,
    x_load, c_load, t_load, x_send, x_recv, h_send, h_recv, e_send, e_recv, r_send, r_recv, o_store,
):
    taps = (pltpu.make_async_copy(taps1, t1, t_sem.at[0]), pltpu.make_async_copy(taps2, t2, t_sem.at[1]))
    for tap in taps:
        tap.start()
    ix, iy = lax.axis_index("gx"), lax.axis_index("gy")
    up, down = lax.rem(ix + gx - 1, gx), lax.rem(ix + 1, gx)
    left, right = lax.rem(iy + gy - 1, gy), lax.rem(iy + 1, gy)
    ids = ({"gx": up}, {"gx": down}, {"gy": left}, {"gy": right})
    barrier = pltpu.get_barrier_semaphore()
    for place in ids:
        pl.semaphore_signal(barrier, inc=1, device_id=place, device_id_type=MESH)

    def load(f, unit):
        start, size = PIECES[unit]
        return pltpu.make_async_copy(
            dens.at[f, pl.ds(start, size)], x.at[f, pl.ds(start + REACH, size)], x_load.at[f, unit]
        )

    def load_cost(unit):
        rows = pl.ds(unit * UNIT, UNIT)
        return pltpu.make_async_copy(cost.at[rows], rc.at[rows], c_load.at[unit])

    def load_term(unit):
        rows = pl.ds(unit * UNIT, UNIT)
        return pltpu.make_async_copy(term.at[rows], tv.at[rows], t_load.at[unit])

    def store(unit):
        rows = pl.ds(pl.multiple_of(unit * UNIT, UNIT), UNIT)
        return pltpu.make_async_copy(tv.at[rows], out.at[rows], o_store.at[unit])

    def remote(src, dst, send, recv, place):
        return pltpu.make_async_remote_copy(
            src_ref=src, dst_ref=dst, send_sem=send, recv_sem=recv, device_id=place, device_id_type=MESH
        )

    def rows_up(f):
        return remote(
            dens.at[f, pl.ds(0, REACH)], x.at[f, pl.ds(REACH + ROWS, REACH)],
            x_send, x_recv.at[f, 0], {"gx": up},
        )

    def rows_down(f):
        return remote(
            dens.at[f, pl.ds(ROWS - REACH, REACH)], x.at[f, pl.ds(0, REACH)],
            x_send, x_recv.at[f, 1], {"gx": down},
        )

    def halo(f, unit, side):
        return remote(
            hs.at[f, unit, side], hr.at[f, unit, side],
            h_send, h_recv.at[f, unit, side], {"gy": (right, left)[side]},
        )

    def edge(n, unit, side):
        return remote(
            es.at[n, unit, side], er.at[n, unit, side],
            e_send, e_recv.at[n, unit, side], {"gy": (right, left)[side]},
        )

    def value_up(n):
        return remote(
            u.at[n, pl.ds(8, 8)], u.at[n, pl.ds(8 + ROWS, 8)], r_send, r_recv.at[n, 0], {"gx": up}
        )

    def value_down(n):
        return remote(
            u.at[n, pl.ds(ROWS, 8)], u.at[n, pl.ds(0, 8)], r_send, r_recv.at[n, 1], {"gx": down}
        )

    def fetch(slot):
        f = STEPS - 1 - slot // UNITS
        for unit in range(UNITS):
            @pl.when((slot + 1) % UNITS == unit)
            def _():
                load(f, unit).start()

    for slot in range(UNITS):
        load(STEPS - 1, (slot + 1) % UNITS).start()
        load_cost((slot + 1) % UNITS).start()
        load_term(slot).start()
    for f in range(STEPS):
        x[f, ROWS + 2 * REACH:, :] = jnp.zeros((32, 128), F32)
    for tap in taps:
        tap.wait()
    build_rows(t1, lhs)
    build_cols(t2, own)
    pl.semaphore_wait(barrier, 4)
    for f in range(STEPS - 1, -1, -1):
        rows_up(f).start()
        rows_down(f).start()

    lane = lax.broadcasted_iota(jnp.int32, (64, 128), 1)
    sub = lax.broadcasted_iota(jnp.int32, (8, 128), 0)

    def blur(f, unit, h):
        base = pl.multiple_of(unit * UNIT + h * HALF, HALF)
        a = b = None
        for group in range(2):
            hi, lo = split(x[f, pl.ds(base + group * 256, 320), :])
            for pair in range(2):
                at = pair * 128
                rhs = jnp.concatenate(
                    [
                        jnp.concatenate([hi[at:at + 128], lo[at:at + 128]], axis=0),
                        jnp.concatenate([hi[at + 64:at + 192], lo[at + 64:at + 192]], axis=0),
                    ],
                    axis=1,
                )
                both = jnp.dot(lhs[...], rhs, preferred_element_type=F32)
                both = both[:64] + both[64:]
                p = 2 * group + pair
                y0, y1 = both[:, :128], both[:, 128:]
                for i, y in enumerate((y0, y1)):
                    hi_y, lo_y = split(y)
                    yb[p * 128 + i * 64:p * 128 + i * 64 + 64, 0:128] = hi_y
                    yb[p * 128 + i * 64:p * 128 + i * 64 + 64, 128:256] = lo_y
                if p == 0:
                    a, b = y0, y1
                else:
                    here = (lane >= 32 * p - 16) & (lane < 32 * p + 16)
                    a = jnp.where(here, pltpu.roll(y0, 32 * p, 1), a)
                    b = jnp.where(here, pltpu.roll(y1, 32 * p, 1), b)
        b = pltpu.roll(b, 16, 1)
        high = lane % 32 >= 16
        at = pl.ds(pl.multiple_of(h * 64, 64), 64)
        hs[f, unit, 0, at, :] = jnp.where(high, a, b)
        hs[f, unit, 1, at, :] = jnp.where(high, b, a)
        for part in range(4):
            o = jnp.dot(yb[part * 128:part * 128 + 128, :], own[...], preferred_element_type=F32)
            o = o[:, :128] + o[:, 128:]
            for k in range(16):
                at = base + part * 128 + k // 8 * 64
                r = rc[pl.ds(at + k % 8, 8, stride=8), :]
                c[f, pl.ds(base + part * 128 + k * 8, 8), :] = o[k * 8:k * 8 + 8] + 0.005 * r

    def send_values(n, unit):
        for b in range(8):
            at = pl.multiple_of(8 + unit * UNIT + b * 128, 8)
            turned = u[n, pl.ds(at, 128), :].T
            es[n, unit, 0, b:b + 1, :] = turned[127:]
            es[n, unit, 1, b:b + 1, :] = turned[:1]
        edge(n, unit, 0).start()
        edge(n, unit, 1).start()

        @pl.when(unit == 0)
        def _():
            value_up(n).start()

        @pl.when(unit == UNITS - 1)
        def _():
            value_down(n).start()

    def start_values(unit):
        for w in range(UNIT // 64):
            at = unit * UNIT + w * 64
            v = jnp.concatenate([tv[pl.ds(at + k, 8, stride=8), :] for k in range(8)], axis=0) * 0.05
            u[0, pl.ds(pl.multiple_of(8 + at, 8), 64), :] = v
        send_values(0, unit)

    def step_half(f, n, unit, h):
        at = pl.ds(pl.multiple_of(h * 64, 64), 64)
        hi, lo = split(jnp.concatenate([hr[f, unit, 0, at, :], hr[f, unit, 1, at, :]], axis=1))
        o = jnp.dot(jnp.concatenate([hi, lo], axis=0), halo_hi[...], preferred_element_type=F32)
        o = o[:64] + o[64:] + jnp.dot(hi, halo_lo[...], preferred_element_type=F32)
        ends = (lane < 16) | (lane >= 112)
        for w in range(8):
            at = pl.multiple_of(unit * UNIT + h * HALF + w * 64, 64)
            p = w // 2
            if w % 2 == 0:
                block = h * 4 + p
                turned = jnp.concatenate(
                    [
                        jnp.broadcast_to(er[n, unit, side, pl.ds(block, 1), :], (64, 128))
                        for side in range(2)
                    ],
                    axis=0,
                ).T
            share = o[:, w % 2 * 128:w % 2 * 128 + 128]
            if p:
                share = pltpu.roll(share, 128 - 32 * p, 1)
            v = u[n, pl.ds(8 + at, 64), :]
            before = u[n, pl.ds(at, 8), :]
            after = u[n, pl.ds(72 + at, 8), :]
            first = jnp.where(sub == 0, pltpu.roll(before, 1, 0), pltpu.roll(v[56:], 1, 0))
            last = jnp.where(sub == 7, pltpu.roll(after, 7, 0), pltpu.roll(v[:8], 7, 0))
            sides = turned[w % 2 * 64:w % 2 * 64 + 64]
            new = v + c[f, pl.ds(at, 64), :] + jnp.where(ends, share, 0.0)
            back = v - jnp.concatenate([first, v[:56]], axis=0)
            new = new - back * jnp.maximum(back + 0.2, 0.2)
            fore = jnp.concatenate([v[8:], last], axis=0) - v
            new = new + fore * jnp.maximum(0.2 - fore, 0.2)
            back = v - jnp.where(lane == 0, sides, pltpu.roll(v, 1, 1))
            new = new - back * jnp.maximum(back + 0.2, 0.2)
            fore = jnp.where(lane == 127, sides, pltpu.roll(v, 127, 1)) - v
            new = new + fore * jnp.maximum(0.2 - fore, 0.2)
            u[n + 1, pl.ds(8 + at, 64), :] = new

    def step(f, n, unit):
        for side in range(2):
            edge(n, unit, side).wait_recv()
            halo(f, unit, side).wait_recv()

        @pl.when(unit == 0)
        def _():
            value_down(n).wait_recv()

        @pl.when(unit == UNITS - 1)
        def _():
            value_up(n).wait_recv()

        step_half(f, n, unit, 0)
        step_half(f, n, unit, 1)

        @pl.when(f > 0)
        def _():
            send_values(n + 1, unit)

        @pl.when(f == 0)
        def _():
            for w in range(UNIT // 64):
                at = unit * UNIT + w * 64
                v = u[STEPS, pl.ds(pl.multiple_of(8 + at, 8), 64), :] * 20.0
                for k in range(8):
                    out[pl.ds(at + k, 8, stride=8), :] = v[k * 8:k * 8 + 8]

    def slot_body(slot, carry):
        @pl.when(slot < SLOTS)
        def _():
            f = STEPS - 1 - slot // UNITS
            unit = (slot + 1) % UNITS

            @pl.when(slot + 4 < SLOTS)
            def _():
                fetch(slot + 4)

            for k in range(UNITS):
                @pl.when(unit == k)
                def _():
                    load(f, k).wait()

            @pl.when(slot < UNITS)
            def _():
                load_cost(unit).wait()
                load_term(slot).wait()

            @pl.when(unit == UNITS - 1)
            def _():
                rows_up(f).wait_recv()

            @pl.when(unit == 0)
            def _():
                rows_down(f).wait_recv()

            def half(h, carry):
                blur(f, unit, h)
                return carry

            half(0, 0)
            half(1, 0)
            halo(f, unit, 0).start()
            halo(f, unit, 1).start()

            @pl.when(slot == 0)
            def _():
                build_halo(t2, halo_hi, halo_lo)

            @pl.when(slot < UNITS)
            def _():
                start_values(slot)

        @pl.when(slot >= LAG)
        def _():
            late = slot - LAG
            n = late // UNITS
            step(STEPS - 1 - n, n, (late + 1) % UNITS)

        return carry

    lax.fori_loop(0, SLOTS + LAG, slot_body, 0)

    remote(x.at[0, pl.ds(0, 128)], x.at[0, pl.ds(0, 128)], x_send, x_recv.at[0, 0], ids[0]).wait_send()
    remote(x.at[0, pl.ds(0, 64)], x.at[0, pl.ds(0, 64)], r_send, r_recv.at[0, 0], ids[0]).wait_send()
    remote(hs, hr, h_send, h_recv.at[0, 0, 0], ids[2]).wait_send()
    remote(es, er, e_send, e_recv.at[0, 0, 0], ids[2]).wait_send()


def solution(mesh):
    gx, gy = mesh.shape["gx"], mesh.shape["gy"]

    def shards(terminal_value, running_cost, density, first_taps, second_taps):
        dma = pltpu.SemaphoreType.DMA
        hbm = pl.BlockSpec(memory_space=pl.ANY)
        return pl.pallas_call(
            functools.partial(kernel, gx, gy),
            name="sweep",
            out_shape=pltpu.VMEM((ROWS, 128), F32),
            in_specs=[hbm] * 5,
            out_specs=pl.BlockSpec(memory_space=pltpu.VMEM),
            scratch_shapes=[
                pltpu.SMEM((TAPS,), F32),
                pltpu.SMEM((TAPS,), F32),
                dma((2,)),
                pltpu.VMEM((STEPS, ROWS + 64, 128), F32),
                pltpu.VMEM((ROWS, 128), F32),
                pltpu.VMEM((ROWS, 128), F32),
                pltpu.VMEM((STEPS + 1, ROWS + 16, 128), F32),
                pltpu.VMEM((STEPS, ROWS, 128), F32),
                pltpu.VMEM((STEPS, UNITS, 2, 128, 128), F32),
                pltpu.VMEM((STEPS, UNITS, 2, 128, 128), F32),
                pltpu.VMEM((STEPS, UNITS, 2, 8, 128), F32),
                pltpu.VMEM((STEPS, UNITS, 2, 8, 128), F32),
                pltpu.VMEM((HALF, 256), BF16),
                pltpu.VMEM((128, 256), BF16),
                pltpu.VMEM((256, 256), BF16),
                pltpu.VMEM((256, 256), BF16),
                pltpu.VMEM((256, 256), BF16),
                dma((STEPS, UNITS)), dma((UNITS,)), dma((UNITS,)),
                dma, dma((STEPS, 2)),
                dma, dma((STEPS, UNITS, 2)),
                dma, dma((STEPS, UNITS, 2)),
                dma, dma((STEPS, 2)),
                dma((UNITS,)),
            ],
            compiler_params=pltpu.CompilerParams(
                collective_id=0, has_side_effects=True, vmem_limit_bytes=60 * 1024 * 1024
            ),
        )(first_taps, second_taps, terminal_value, running_cost, density)

    placed = (P("gx", "gy"), P("gx", "gy"), P(None, "gx", "gy"), P(), P())
    return jax.shard_map(shards, mesh=mesh, in_specs=placed, out_specs=P("gx", "gy"), check_vma=False)
```

```python
import functools

import jax
import jax.numpy as jnp
from jax import lax
from jax.experimental import pallas as pl
from jax.experimental.pallas import tpu as pltpu
from jax.sharding import PartitionSpec as P

MESH = pl.DeviceIdType.MESH
F32 = jnp.float32
BF16 = jnp.bfloat16
STEPS = 4
ROWS = 4096
UNIT = 1024
UNITS = ROWS // UNIT
HALF = 512
TAPS = 33
REACH = 16
LAG = 4
SLOTS = STEPS * UNITS
PIECES = ((0, 1008), (1008, 1088), (2096, 1024), (3120, 976))


def split(x):
    hi = x.astype(BF16)
    lo = (x - hi.astype(F32)).astype(BF16)
    return hi, lo


def toeplitz(index, taps_ref, first, last, scale):
    def add(t, acc):
        return jnp.where(index == t, taps_ref[t] * scale, acc)

    return lax.fori_loop(first, last, add, jnp.zeros(index.shape, F32))


def band(index, taps_ref, scale):
    acc = jnp.zeros(index.shape, F32)
    for t in range(TAPS):
        acc = jnp.where(index == t, taps_ref[t] * scale, acc)
    return acc


def build_rows(taps_ref, lhs):
    pos = lax.broadcasted_iota(jnp.int32, (64, 128), 0)
    col = lax.broadcasted_iota(jnp.int32, (64, 128), 1)
    row = (pos % 8) * 8 + pos // 8
    hi, lo = split(band(col - row, taps_ref, 1.0))
    lhs[0:64, 0:128] = hi
    lhs[0:64, 128:256] = hi
    lhs[64:128, 0:128] = lo
    lhs[64:128, 128:256] = jnp.zeros((64, 128), BF16)


def build_cols(taps_ref, own):
    src = lax.broadcasted_iota(jnp.int32, (128, 128), 0)
    dst = lax.broadcasted_iota(jnp.int32, (128, 128), 1)
    hi, lo = split(band(src - dst + REACH, taps_ref, 0.005))
    own[0:128, 0:128] = hi
    own[0:128, 128:256] = lo
    own[128:256, 0:128] = hi
    own[128:256, 128:256] = jnp.zeros((128, 128), BF16)


def build_halo(taps_ref, halo_hi, halo_lo):
    lam = lax.broadcasted_iota(jnp.int32, (128, 256), 0)
    nu = lax.broadcasted_iota(jnp.int32, (128, 256), 1)
    out_part = nu // 128
    place = (nu % 128 + 16) % 128
    out_q, out_e = place // 32, place % 32
    upper = lam % 32 >= 16
    shifted = (lam + 16) % 128
    q = jnp.where(upper, shifted // 32, lam // 32)
    m = jnp.where(upper, shifted % 32, lam % 32)
    part = jnp.where(upper, 0, 1)
    fits = (part == out_part) & (q == out_q) & (out_e >= 16)
    index = jnp.where(fits, m - (out_e - 16), -1)
    hi, lo = split(toeplitz(index, taps_ref, 0, 16, 0.005))
    halo_hi[0:128, :] = hi
    halo_lo[0:128, :] = lo
    m = jnp.where(upper, lam % 32 - 16, lam % 32)
    part = jnp.where(upper, 1, 0)
    fits = (part == out_part) & (lam // 32 == out_q) & (out_e < 16)
    index = jnp.where(fits, 32 + m - out_e, -1)
    hi, lo = split(toeplitz(index, taps_ref, 17, TAPS, 0.005))
    halo_hi[128:256, :] = hi
    halo_lo[128:256, :] = lo


def kernel(
    gx, gy, taps1, taps2, term, cost, dens, out, t1, t2, t_sem,
    x, rc, tv, u, c, hs, hr, es, er, yb, lhs, own, halo_hi, halo_lo,
    x_load, c_load, t_load, x_send, x_recv, h_send, h_recv, e_send, e_recv, r_send, r_recv, o_store,
):
    taps = (pltpu.make_async_copy(taps1, t1, t_sem.at[0]), pltpu.make_async_copy(taps2, t2, t_sem.at[1]))
    for tap in taps:
        tap.start()
    ix, iy = lax.axis_index("gx"), lax.axis_index("gy")
    up, down = lax.rem(ix + gx - 1, gx), lax.rem(ix + 1, gx)
    left, right = lax.rem(iy + gy - 1, gy), lax.rem(iy + 1, gy)
    ids = ({"gx": up}, {"gx": down}, {"gy": left}, {"gy": right})
    barrier = pltpu.get_barrier_semaphore()
    for place in ids:
        pl.semaphore_signal(barrier, inc=1, device_id=place, device_id_type=MESH)

    def load(f, unit):
        start, size = PIECES[unit]
        return pltpu.make_async_copy(
            dens.at[f, pl.ds(start, size)], x.at[f, pl.ds(start + REACH, size)], x_load.at[f, unit]
        )

    def load_cost(unit):
        rows = pl.ds(unit * UNIT, UNIT)
        return pltpu.make_async_copy(cost.at[rows], rc.at[rows], c_load.at[unit])

    def load_term(unit):
        rows = pl.ds(unit * UNIT, UNIT)
        return pltpu.make_async_copy(term.at[rows], tv.at[rows], t_load.at[unit])

    def store(unit):
        rows = pl.ds(pl.multiple_of(unit * UNIT, UNIT), UNIT)
        return pltpu.make_async_copy(tv.at[rows], out.at[rows], o_store.at[unit])

    def remote(src, dst, send, recv, place):
        return pltpu.make_async_remote_copy(
            src_ref=src, dst_ref=dst, send_sem=send, recv_sem=recv, device_id=place, device_id_type=MESH
        )

    def rows_up(f):
        return remote(
            dens.at[f, pl.ds(0, REACH)], x.at[f, pl.ds(REACH + ROWS, REACH)],
            x_send, x_recv.at[f, 0], {"gx": up},
        )

    def rows_down(f):
        return remote(
            dens.at[f, pl.ds(ROWS - REACH, REACH)], x.at[f, pl.ds(0, REACH)],
            x_send, x_recv.at[f, 1], {"gx": down},
        )

    def halo(f, unit, side):
        return remote(
            hs.at[f, unit, side], hr.at[f, unit, side],
            h_send, h_recv.at[f, unit, side], {"gy": (right, left)[side]},
        )

    def edge(n, unit, side):
        return remote(
            es.at[n, unit, side], er.at[n, unit, side],
            e_send, e_recv.at[n, unit, side], {"gy": (right, left)[side]},
        )

    def value_up(n):
        return remote(
            u.at[n, pl.ds(8, 8)], u.at[n, pl.ds(8 + ROWS, 8)], r_send, r_recv.at[n, 0], {"gx": up}
        )

    def value_down(n):
        return remote(
            u.at[n, pl.ds(ROWS, 8)], u.at[n, pl.ds(0, 8)], r_send, r_recv.at[n, 1], {"gx": down}
        )

    def fetch(slot):
        f = STEPS - 1 - slot // UNITS
        for unit in range(UNITS):
            @pl.when((slot + 1) % UNITS == unit)
            def _():
                load(f, unit).start()

    for slot in range(UNITS):
        load(STEPS - 1, (slot + 1) % UNITS).start()
        load_cost((slot + 1) % UNITS).start()
        load_term(slot).start()
    for f in range(STEPS):
        x[f, ROWS + 2 * REACH:, :] = jnp.zeros((32, 128), F32)
    for tap in taps:
        tap.wait()
    build_rows(t1, lhs)
    build_cols(t2, own)
    pl.semaphore_wait(barrier, 4)
    for f in range(STEPS - 1, -1, -1):
        rows_up(f).start()
        rows_down(f).start()

    lane = lax.broadcasted_iota(jnp.int32, (64, 128), 1)
    sub = lax.broadcasted_iota(jnp.int32, (8, 128), 0)

    def blur(f, unit, h):
        base = pl.multiple_of(unit * UNIT + h * HALF, HALF)
        a = b = None
        for group in range(2):
            hi, lo = split(x[f, pl.ds(base + group * 256, 320), :])
            for pair in range(2):
                at = pair * 128
                rhs = jnp.concatenate(
                    [
                        jnp.concatenate([hi[at:at + 128], lo[at:at + 128]], axis=0),
                        jnp.concatenate([hi[at + 64:at + 192], lo[at + 64:at + 192]], axis=0),
                    ],
                    axis=1,
                )
                both = jnp.dot(lhs[...], rhs, preferred_element_type=F32)
                both = both[:64] + both[64:]
                p = 2 * group + pair
                y0, y1 = both[:, :128], both[:, 128:]
                for i, y in enumerate((y0, y1)):
                    hi_y, lo_y = split(y)
                    yb[p * 128 + i * 64:p * 128 + i * 64 + 64, 0:128] = hi_y
                    yb[p * 128 + i * 64:p * 128 + i * 64 + 64, 128:256] = lo_y
                if p == 0:
                    a, b = y0, y1
                else:
                    here = (lane >= 32 * p - 16) & (lane < 32 * p + 16)
                    a = jnp.where(here, pltpu.roll(y0, 32 * p, 1), a)
                    b = jnp.where(here, pltpu.roll(y1, 32 * p, 1), b)
        b = pltpu.roll(b, 16, 1)
        high = lane % 32 >= 16
        at = pl.ds(pl.multiple_of(h * 64, 64), 64)
        hs[f, unit, 0, at, :] = jnp.where(high, a, b)
        hs[f, unit, 1, at, :] = jnp.where(high, b, a)
        for part in range(4):
            o = jnp.dot(yb[part * 128:part * 128 + 128, :], own[...], preferred_element_type=F32)
            o = o[:, :128] + o[:, 128:]
            for k in range(16):
                at = base + part * 128 + k // 8 * 64
                r = rc[pl.ds(at + k % 8, 8, stride=8), :]
                c[f, pl.ds(base + part * 128 + k * 8, 8), :] = o[k * 8:k * 8 + 8] + 0.005 * r

    def send_values(n, unit):
        for b in range(8):
            at = pl.multiple_of(8 + unit * UNIT + b * 128, 8)
            turned = u[n, pl.ds(at, 128), :].T
            es[n, unit, 0, b:b + 1, :] = turned[127:]
            es[n, unit, 1, b:b + 1, :] = turned[:1]
        edge(n, unit, 0).start()
        edge(n, unit, 1).start()

        @pl.when(unit == 0)
        def _():
            value_up(n).start()

        @pl.when(unit == UNITS - 1)
        def _():
            value_down(n).start()

    def start_values(unit):
        for w in range(UNIT // 64):
            at = unit * UNIT + w * 64
            v = jnp.concatenate([tv[pl.ds(at + k, 8, stride=8), :] for k in range(8)], axis=0) * 0.05
            u[0, pl.ds(pl.multiple_of(8 + at, 8), 64), :] = v
        send_values(0, unit)

    def step_half(f, n, unit, h):
        at = pl.ds(pl.multiple_of(h * 64, 64), 64)
        hi, lo = split(jnp.concatenate([hr[f, unit, 0, at, :], hr[f, unit, 1, at, :]], axis=1))
        o = jnp.dot(jnp.concatenate([hi, lo], axis=0), halo_hi[...], preferred_element_type=F32)
        o = o[:64] + o[64:] + jnp.dot(hi, halo_lo[...], preferred_element_type=F32)
        ends = (lane < 16) | (lane >= 112)
        for w in range(8):
            at = pl.multiple_of(unit * UNIT + h * HALF + w * 64, 64)
            p = w // 2
            if w % 2 == 0:
                block = h * 4 + p
                turned = jnp.concatenate(
                    [
                        jnp.broadcast_to(er[n, unit, side, pl.ds(block, 1), :], (64, 128))
                        for side in range(2)
                    ],
                    axis=0,
                ).T
            share = o[:, w % 2 * 128:w % 2 * 128 + 128]
            if p:
                share = pltpu.roll(share, 128 - 32 * p, 1)
            v = u[n, pl.ds(8 + at, 64), :]
            before = u[n, pl.ds(at, 8), :]
            after = u[n, pl.ds(72 + at, 8), :]
            first = jnp.where(sub == 0, pltpu.roll(before, 1, 0), pltpu.roll(v[56:], 1, 0))
            last = jnp.where(sub == 7, pltpu.roll(after, 7, 0), pltpu.roll(v[:8], 7, 0))
            sides = turned[w % 2 * 64:w % 2 * 64 + 64]
            new = v + c[f, pl.ds(at, 64), :] + jnp.where(ends, share, 0.0)
            back = v - jnp.concatenate([first, v[:56]], axis=0)
            new = new - back * jnp.maximum(back + 0.2, 0.2)
            fore = jnp.concatenate([v[8:], last], axis=0) - v
            new = new + fore * jnp.maximum(0.2 - fore, 0.2)
            back = v - jnp.where(lane == 0, sides, pltpu.roll(v, 1, 1))
            new = new - back * jnp.maximum(back + 0.2, 0.2)
            fore = jnp.where(lane == 127, sides, pltpu.roll(v, 127, 1)) - v
            new = new + fore * jnp.maximum(0.2 - fore, 0.2)
            u[n + 1, pl.ds(8 + at, 64), :] = new

    def step(f, n, unit):
        for side in range(2):
            edge(n, unit, side).wait_recv()
            halo(f, unit, side).wait_recv()

        @pl.when(unit == 0)
        def _():
            value_down(n).wait_recv()

        @pl.when(unit == UNITS - 1)
        def _():
            value_up(n).wait_recv()

        step_half(f, n, unit, 0)
        step_half(f, n, unit, 1)

        @pl.when(f > 0)
        def _():
            send_values(n + 1, unit)

        @pl.when(f == 0)
        def _():
            for w in range(UNIT // 64):
                at = unit * UNIT + w * 64
                v = u[STEPS, pl.ds(pl.multiple_of(8 + at, 8), 64), :] * 20.0
                for k in range(8):
                    out[pl.ds(at + k, 8, stride=8), :] = v[k * 8:k * 8 + 8]

    def slot_body(slot, carry):
        @pl.when(slot < SLOTS)
        def _():
            f = STEPS - 1 - slot // UNITS
            unit = (slot + 1) % UNITS

            @pl.when(slot + 4 < SLOTS)
            def _():
                fetch(slot + 4)

            for k in range(UNITS):
                @pl.when(unit == k)
                def _():
                    load(f, k).wait()

            @pl.when(slot < UNITS)
            def _():
                load_cost(unit).wait()
                load_term(slot).wait()

            @pl.when(unit == UNITS - 1)
            def _():
                rows_up(f).wait_recv()

            @pl.when(unit == 0)
            def _():
                rows_down(f).wait_recv()

            def half(h, carry):
                blur(f, unit, h)
                return carry

            half(0, 0)
            half(1, 0)
            halo(f, unit, 0).start()
            halo(f, unit, 1).start()

            @pl.when(slot == 0)
            def _():
                build_halo(t2, halo_hi, halo_lo)

            @pl.when(slot < UNITS)
            def _():
                start_values(slot)

        @pl.when(slot >= LAG)
        def _():
            late = slot - LAG
            n = late // UNITS
            step(STEPS - 1 - n, n, (late + 1) % UNITS)

        return carry

    lax.fori_loop(0, SLOTS + LAG, slot_body, 0)

    remote(x.at[0, pl.ds(0, 128)], x.at[0, pl.ds(0, 128)], x_send, x_recv.at[0, 0], ids[0]).wait_send()
    remote(x.at[0, pl.ds(0, 64)], x.at[0, pl.ds(0, 64)], r_send, r_recv.at[0, 0], ids[0]).wait_send()
    remote(hs, hr, h_send, h_recv.at[0, 0, 0], ids[2]).wait_send()
    remote(es, er, e_send, e_recv.at[0, 0, 0], ids[2]).wait_send()


def solution(mesh):
    gx, gy = mesh.shape["gx"], mesh.shape["gy"]

    def shards(terminal_value, running_cost, density, first_taps, second_taps):
        dma = pltpu.SemaphoreType.DMA
        hbm = pl.BlockSpec(memory_space=pl.ANY)
        return pl.pallas_call(
            functools.partial(kernel, gx, gy),
            name="sweep",
            out_shape=pltpu.VMEM((ROWS, 128), F32),
            in_specs=[hbm] * 5,
            out_specs=pl.BlockSpec(memory_space=pltpu.VMEM),
            scratch_shapes=[
                pltpu.SMEM((TAPS,), F32),
                pltpu.SMEM((TAPS,), F32),
                dma((2,)),
                pltpu.VMEM((STEPS, ROWS + 64, 128), F32),
                pltpu.VMEM((ROWS, 128), F32),
                pltpu.VMEM((ROWS, 128), F32),
                pltpu.VMEM((STEPS + 1, ROWS + 16, 128), F32),
                pltpu.VMEM((STEPS, ROWS, 128), F32),
                pltpu.VMEM((STEPS, UNITS, 2, 128, 128), F32),
                pltpu.VMEM((STEPS, UNITS, 2, 128, 128), F32),
                pltpu.VMEM((STEPS, UNITS, 2, 8, 128), F32),
                pltpu.VMEM((STEPS, UNITS, 2, 8, 128), F32),
                pltpu.VMEM((HALF, 256), BF16),
                pltpu.VMEM((128, 256), BF16),
                pltpu.VMEM((256, 256), BF16),
                pltpu.VMEM((256, 256), BF16),
                pltpu.VMEM((256, 256), BF16),
                dma((STEPS, UNITS)), dma((UNITS,)), dma((UNITS,)),
                dma, dma((STEPS, 2)),
                dma, dma((STEPS, UNITS, 2)),
                dma, dma((STEPS, UNITS, 2)),
                dma, dma((STEPS, 2)),
                dma((UNITS,)),
            ],
            compiler_params=pltpu.CompilerParams(
                collective_id=0, has_side_effects=True, vmem_limit_bytes=60 * 1024 * 1024
            ),
        )(first_taps, second_taps, terminal_value, running_cost, density)

    placed = (P("gx", "gy"), P("gx", "gy"), P(None, "gx", "gy"), P(), P())
    return jax.shard_map(shards, mesh=mesh, in_specs=placed, out_specs=P("gx", "gy"), check_vma=False)
```
